32 devices in a mesh: shard: 8 (over z, y), rep: 4 (over x, core).
Axes of the slice: x: 2, y: 2, z: 4, core: 2. Of those that a mesh axis runs over, the one named last changes fastest.
Arguments:
- tokens: bfloat16 [4096, 768], P(('shard', 'rep')), may hold values from -6 to 6
- labels: int32 [4096], P(('shard', 'rep')), may hold values from 0 to 3, as said below
- w_qkv: bfloat16 [768, 2304], P('shard'), may hold values from -0.21875 to 0.21875
- bias_qv: bfloat16 [1536], P('shard'), may hold values from -3 to 3
- w_out: bfloat16 [768, 768], P('shard'), may hold values from -0.875 to 0.875
- bias_out: bfloat16 [768], P('shard'), may hold values from -3 to 3
- w_in: bfloat16 [768, 3072], P('shard'), may hold values from -0.21875 to 0.21875
- bias_in: bfloat16 [3072], P('shard'), may hold values from -3 to 3
- w_back: bfloat16 [3072, 768], P('shard'), may hold values from -0.109375 to 0.109375
- bias_back: bfloat16 [768], P('shard'), may hold values from -3 to 3
- gain_one: bfloat16 [768], P('shard'), may hold values from 0.099609375 to 1.8984375
- shift_one: bfloat16 [768], P('shard'), may hold values from -3 to 3
- gain_two: bfloat16 [768], P('shard'), may hold values from 0.099609375 to 1.8984375
- shift_two: bfloat16 [768], P('shard'), may hold values from -3 to 3
- cotangent: bfloat16 [4096, 768], P(('shard', 'rep')), may hold values from -6 to 6
Outputs:
- output: bfloat16 [4096, 768], P(('shard', 'rep'))
- grad_tokens: float32 [4096, 768], P(('shard', 'rep'))
- grad_w_qkv: float32 [768, 2304], P('shard')
- grad_bias_qv: float32 [1536], P('shard')
- grad_w_out: float32 [768, 768], P('shard')
- grad_bias_out: float32 [768], P('shard')
- grad_w_in: float32 [768, 3072], P('shard')
- grad_bias_in: float32 [3072], P('shard')
- grad_w_back: float32 [3072, 768], P('shard')
- grad_bias_back: float32 [768], P('shard')
- grad_gain_one: float32 [768], P('shard')
- grad_shift_one: float32 [768], P('shard')
- grad_gain_two: float32 [768], P('shard')
- grad_shift_two: float32 [768], P('shard')
The draws below stay inside these ranges and needn't reach their ends.
Inputs may be any that keep to these rules, and one draw needn't show every extreme that they name: `labels`: within each block of 128 slots of one device, live tokens come first and number at least 85; each positive label marks one sequence, a contiguous run, at most 3 on a device; one device holds a single sequence of all 128 slots.
All inputs are finite; a program needn't handle non-finite values.
Results may differ from the reference program's by a relative error of at most 0.012.
The reference program's roundings to bfloat16 on the way count: a program that leaves them out, or rounds other values in their place, can miss the bound.
Values may be sent and summed in bfloat16 or wider, within the bound.
A program may use at most 128 MiB of HBM per device.

```python
import math
import jax
import jax.numpy as jnp
from jax import lax

D = 768
HEADS = 12
HEAD_DIM = 64
FF = 3072
CAP = 128
DOCS_DEV = 3
MIN_LIVE = 85
TOKENS = 4096
N_SHARD = 8


def draw_labels(key, part):
    key = jax.random.fold_in(key, 7)
    devices = TOKENS // CAP
    count_key, longest_key, boundary_key = jax.random.split(key, 3)
    live_count = jax.random.randint(count_key, (devices,), MIN_LIVE, CAP)
    longest = jax.random.randint(longest_key, (), 0, devices)
    slot_index = jnp.arange(devices)
    live_count = jnp.where(slot_index == longest, CAP, live_count)
    boundary = jax.random.randint(boundary_key, (devices, DOCS_DEV - 1), 1, MIN_LIVE)
    boundary = jnp.where((slot_index == longest)[:, None], CAP, boundary)
    position = jnp.arange(CAP)
    doc_label = 1 + jnp.sum((position[None, :, None] >= boundary[:, None, :]).astype(jnp.int32), -1)
    doc_label = jnp.where(position[None, :] < live_count[:, None], doc_label, 0)
    return doc_label.reshape(-1).astype(jnp.int32)


def shard_levels(own_key, extent, shards, least, high):
    factor_of = 1.0
    for dim, parts in shards:
        draws = jax.random.uniform(jax.random.fold_in(jax.random.fold_in(own_key, 6), dim), (parts,), jnp.float32, least / len(shards), high / len(shards))
        factor_of = factor_of * jnp.repeat(jnp.exp(draws), extent[dim] // parts).reshape((-1,) + (1,) * (len(extent) - 1 - dim))
    return factor_of


def gaussian(key, extent, scale, limit, cuts=(), kind=jnp.bfloat16):
    gain = shard_levels(key, extent, cuts, -0.22, 0.18) if cuts else 1.0
    entries = jax.random.normal(key, extent, jnp.float32) * scale * gain
    return jnp.minimum(jnp.maximum(entries, -limit), limit).astype(kind)


def setup_inputs(seed: int = 0) -> dict:
    seeds = jax.random.split(jax.random.key(seed), 16)
    tokens = gaussian(seeds[0], (TOKENS, D), 1.0, 6.0, ((0, 32),))
    labels = draw_labels(jax.random.fold_in(seeds[15], 71), 0)
    w_qkv = gaussian(seeds[2], (D, 3 * D), D ** -0.5, 0.21875, ((0, 8),))
    bias_qv = gaussian(seeds[3], (2 * D,), 0.5, 3.0, ((0, 8),))
    w_out = gaussian(seeds[4], (D, D), (D // 16) ** -0.5, 0.875, ((0, 8),))
    bias_out = gaussian(seeds[5], (D,), 0.5, 3.0, ((0, 8),))
    w_in = gaussian(seeds[6], (D, FF), D ** -0.5, 0.21875, ((0, 8),))
    bias_in = gaussian(seeds[7], (FF,), 0.5, 3.0, ((0, 8),))
    w_back = gaussian(seeds[8], (FF, D), FF ** -0.5, 0.109375, ((0, 8),))
    bias_back = gaussian(seeds[9], (D,), 0.5, 3.0, ((0, 8),))
    gain_one = jnp.clip(1.0 + 0.18 * jax.random.normal(seeds[10], (D,), jnp.float32), 0.099609375, 1.8984375).astype(jnp.bfloat16)
    shift_one = gaussian(seeds[11], (D,), 0.5, 3.0, ((0, 8),))
    gain_two = jnp.clip(1.0 + 0.18 * jax.random.normal(seeds[12], (D,), jnp.float32), 0.099609375, 1.8984375).astype(jnp.bfloat16)
    shift_two = gaussian(seeds[13], (D,), 0.5, 3.0, ((0, 8),))
    cotangent = gaussian(seeds[14], (TOKENS, D), 1.0, 6.0, ((0, 32),))
    return {"tokens": tokens, "labels": labels, "w_qkv": w_qkv, "bias_qv": bias_qv, "w_out": w_out, "bias_out": bias_out, "w_in": w_in, "bias_in": bias_in, "w_back": w_back, "bias_back": bias_back, "gain_one": gain_one, "shift_one": shift_one, "gain_two": gain_two, "shift_two": shift_two, "cotangent": cotangent}


EPSILON = 1e-05
PRECISE = lax.Precision.HIGHEST

@jax.custom_vjp
def low(v):
    return lax.optimization_barrier(v.astype(jnp.bfloat16)).astype(jnp.float32)

@jax.custom_vjp
def low_back(v):
    return v

def low_keep(v):
    return (low(v), None)

def low_pass(kept, grad):
    return (grad,)

def back_keep(v):
    return (v, None)

def back_low(kept, grad):
    return (low(grad),)
low.defvjp(low_keep, low_pass)
low_back.defvjp(back_keep, back_low)

def normalize(summed, gain_row, shift_row):
    average = lax.optimization_barrier(jnp.mean(summed, -1, keepdims=True))
    centred = summed - average
    variance = lax.optimization_barrier(jnp.mean(centred * centred, -1, keepdims=True))
    return centred * lax.rsqrt(variance + EPSILON) * gain_row + shift_row

def group_layer(weights, input_rows, doc_labels):
    w_qkv, bias_qv, w_out, bias_out, w_in, bias_in, w_back, bias_back, gain_one, shift_one, gain_two, shift_two = weights
    model_width = w_out.shape[0]
    qkv = jnp.dot(input_rows, w_qkv, precision=PRECISE)
    query_rows = low_back(low(qkv[:, :model_width] + bias_qv[:model_width]))
    key_rows = low_back(low(qkv[:, model_width:2 * model_width]))
    value_rows = low_back(low(qkv[:, 2 * model_width:] + bias_qv[model_width:]))
    slot_count = input_rows.shape[0] // CAP

    def split_heads(matrix):
        return matrix.reshape(slot_count, CAP, HEADS, HEAD_DIM)
    score_scale = 1.0 / math.sqrt(HEAD_DIM)
    scores = jnp.einsum('sqhd,skhd->shqk', split_heads(query_rows), split_heads(key_rows), precision=PRECISE) * score_scale
    scores = low_back(scores)
    slot_labels = doc_labels.reshape(slot_count, CAP)
    same_doc = slot_labels[:, None, :, None] == slot_labels[:, None, None, :]
    scores = jnp.where(same_doc, scores, -1000000000.0)
    highest = lax.optimization_barrier(jnp.max(scores, -1, keepdims=True))
    exponent = jnp.exp(scores - highest)
    attention = exponent / lax.optimization_barrier(jnp.sum(exponent, -1, keepdims=True))
    mixed_heads = jnp.einsum('shqk,skhd->sqhd', low(attention), split_heads(value_rows), precision=PRECISE)
    mixed_heads = low_back(low(mixed_heads.reshape(-1, model_width)))
    attn_out = low_back(jnp.dot(mixed_heads, w_out, precision=PRECISE) + bias_out)
    first_out = normalize(input_rows + attn_out, gain_one, shift_one)
    inner_sum = low_back(jnp.dot(low(first_out), w_in, precision=PRECISE) + bias_in)
    activated = low(jax.nn.gelu(inner_sum, approximate=False))
    branch = low_back(jnp.dot(activated, w_back, precision=PRECISE) + bias_back)
    final_out = normalize(first_out + branch, gain_two, shift_two)
    live_rows = (doc_labels > 0).astype(final_out.dtype)[:, None]
    return final_out * live_rows

def reference(tokens, labels, w_qkv, bias_qv, w_out, bias_out, w_in, bias_in, w_back, bias_back, gain_one, shift_one, gain_two, shift_two, cotangent):
    params = tuple((p.astype(jnp.float32) for p in (w_qkv, bias_qv, w_out, bias_out, w_in, bias_in, w_back, bias_back, gain_one, shift_one, gain_two, shift_two)))
    groups = N_SHARD
    input_rows = tokens.astype(jnp.float32).reshape(groups, -1, D)
    doc_groups = labels.reshape(groups, -1)
    checked = jax.checkpoint(group_layer)

    def forward(weights, inputs):
        return lax.map(lambda pair_rows: checked(weights, pair_rows[0], pair_rows[1]), (inputs, doc_groups))
    result, pull_back = jax.vjp(forward, params, input_rows)
    grad_params, grad_rows = pull_back(cotangent.astype(jnp.float32).reshape(groups, -1, D))
    return (result.reshape(-1, D).astype(jnp.bfloat16), grad_rows.reshape(-1, D), grad_params[0], grad_params[1], grad_params[2], grad_params[3], grad_params[4], grad_params[5], grad_params[6], grad_params[7], grad_params[8], grad_params[9], grad_params[10], grad_params[11])
```

```python
import functools
import math

import jax
import jax.numpy as jnp
from jax import lax
from jax.experimental import pallas as pl
from jax.experimental.pallas import tpu as pltpu
from jax.sharding import PartitionSpec as P

HEADS = 12
HEAD_DIM = 64
EPSILON = 1e-05
MESH = pl.DeviceIdType.MESH
QUAD = 4


class Place:
    def __init__(self, n_shard):
        self.n = n_shard
        self.half = n_shard // 2
        self.s = lax.axis_index("shard")
        self.r = lax.axis_index("rep")
        self.base = self.r - self.r % QUAD
        self.x = (self.r % QUAD) // 2
        self.c = self.r % 2
        z, y = self.s // 2, self.s % 2
        self.p = z * (1 - y) + (n_shard - 1 - z) * y
        self.core_peer = (self.s, self.base + self.x * 2 + (1 - self.c))
        self.chip_peer = (self.s, self.base + (1 - self.x) * 2 + self.c)
        self.right = (self.at(1), self.r)
        self.left = (self.at(-1), self.r)

    def at(self, offset):
        p = (self.p + offset + 2 * self.n) % self.n
        upper = p // self.half
        return (1 - upper) * 2 * p + upper * (2 * (self.n - 1 - p) + 1)

    def greet(self):
        barrier = pltpu.get_barrier_semaphore()
        targets = [((self.s + k) % self.n, self.r) for k in range(1, self.n)]
        targets += [self.core_peer, self.chip_peer]
        for device in targets:
            pl.semaphore_signal(barrier, inc=1, device_id=device, device_id_type=MESH)
        pl.semaphore_wait(barrier, len(targets))


def remote(src, dst, send, recv, device):
    return pltpu.make_async_remote_copy(
        src_ref=src,
        dst_ref=dst,
        send_sem=send,
        recv_sem=recv,
        device_id=device,
        device_id_type=MESH,
    )


def cols(index, width):
    return pl.ds(pl.multiple_of(index * width, 128), width)


def hops(n, unit):
    more, less = n // 2, n - 1 - n // 2
    return (more, less) if unit == 0 else (less, more)


def gather_kernel(n, *refs):
    ins, outs = refs[:5], refs[5:10]
    own_sem, ring_s, ring_r, chip_s, chip_r, core_s, core_r, far_s, far_r, small_s, small_r = refs[10:]
    me = Place(n)
    widths = (outs[0].shape[2] // 2, outs[1].shape[2] // 2, outs[2].shape[2] // 4)

    def part(k, block, x):
        if k < 2:
            return outs[k].at[block, :, cols(me.c, widths[k])]
        if k == 2:
            return outs[2].at[block, :, cols(me.c * 2 + x, widths[2])]
        return outs[3].at[block, me.c * 2 + x]

    def mine(k):
        if k < 2:
            return ins[k].at[:, cols(me.c, widths[k])]
        if k == 2:
            return ins[2].at[:, cols(me.c * 2 + me.x, widths[2])]
        return ins[3].at[me.c * 2 + me.x]

    me.greet()
    pending = []

    def ring(k, way, t):
        block = me.at(-t if way == 0 else t)
        src = mine(k) if t == 0 else part(k, block, me.x)
        copy = remote(
            src,
            part(k, block, me.x),
            ring_s.at[k, way, t],
            ring_r.at[k, way, t],
            me.right if way == 0 else me.left,
        )
        copy.start()
        pending.append(copy)

    def from_ring(k, way, t):
        block = me.at(-1 - t if way == 0 else 1 + t)
        here = part(k, block, me.x)
        remote(here, here, ring_s.at[k, way, t], ring_r.at[k, way, t], me.left).wait_recv()
        return block

    def to_peer(k, block, x, send, recv, device):
        copy = remote(part(k, block, x), part(k, block, x), send, recv, device)
        copy.start()
        pending.append(copy)

    order = (2, 3, 0, 1)
    for k in order:
        for way in range(2):
            ring(k, way, 0)
    for j in range(1, n):
        other = (me.s + j) % n
        copy = remote(ins[4], outs[4].at[me.s], small_s.at[j], small_r.at[j], (other, me.r))
        copy.start()
        pending.append(copy)
    own = [
        pltpu.make_async_copy(ins[k], outs[k].at[me.s], own_sem.at[k]) for k in range(5)
    ]
    for copy in own:
        copy.start()

    def from_chip(k, way, t):
        block = me.at(-1 - t if way == 0 else 1 + t)
        here = part(k, block, 1 - me.x)
        i = k - 2
        remote(here, here, chip_s.at[i, way, t], chip_r.at[i, way, t], me.chip_peer).wait_recv()
        to_peer(k, block, 1 - me.x, far_s.at[i, way, t], far_r.at[i, way, t], me.core_peer)

    most = n // 2
    for t in range(most + 1):
        for k in order:
            unit = 1 if k > 1 else 0
            for way in range(2):
                last = hops(n, unit)[way]
                if t < last:
                    block = from_ring(k, way, t)
                    if t + 1 < last:
                        ring(k, way, t + 1)
                    if unit:
                        to_peer(
                            k,
                            block,
                            me.x,
                            chip_s.at[k - 2, way, t],
                            chip_r.at[k - 2, way, t],
                            me.chip_peer,
                        )
                    to_peer(
                        k, block, me.x, core_s.at[k, way, t], core_r.at[k, way, t], me.core_peer
                    )
        for k in (2, 3):
            for way in range(2):
                if 0 <= t - 1 < hops(n, 1)[way]:
                    from_chip(k, way, t - 1)

    def peer_part(k, block, x):
        if k < 2:
            return outs[k].at[block, :, cols(1 - me.c, widths[k])]
        if k == 2:
            return outs[2].at[block, :, cols((1 - me.c) * 2 + x, widths[2])]
        return outs[3].at[block, (1 - me.c) * 2 + x]

    for k in range(4):
        unit = 1 if k > 1 else 0
        for way in range(2):
            for t in range(hops(n, unit)[way]):
                block = me.at(-1 - t if way == 0 else 1 + t)
                here = peer_part(k, block, me.x)
                remote(
                    here, here, core_s.at[k, way, t], core_r.at[k, way, t], me.core_peer
                ).wait_recv()
                if unit:
                    here = peer_part(k, block, 1 - me.x)
                    i = k - 2
                    remote(
                        here, here, far_s.at[i, way, t], far_r.at[i, way, t], me.core_peer
                    ).wait_recv()
    for j in range(1, n):
        here = outs[4].at[(me.s + n - j) % n]
        remote(here, here, small_s.at[j], small_r.at[j], me.core_peer).wait_recv()
    for copy in pending:
        copy.wait_send()
    for copy in own:
        copy.wait()


def gather_weights(n, w_qkv, w_out, w_in, w_back, small):
    rows = w_qkv.shape[0]
    w_back = w_back.reshape(4, rows, w_back.shape[1])
    operands = (w_qkv, w_out, w_in, w_back, small)
    most = n // 2
    dma = pltpu.SemaphoreType.DMA
    full = pl.pallas_call(
        functools.partial(gather_kernel, n),
        out_shape=[jax.ShapeDtypeStruct((n,) + a.shape, a.dtype) for a in operands],
        in_specs=[pl.BlockSpec(memory_space=pl.ANY)] * 5,
        out_specs=[pl.BlockSpec(memory_space=pl.ANY)] * 5,
        scratch_shapes=[dma((5,))]
        + [dma((4, 2, most))] * 2
        + [dma((2, 2, most))] * 2
        + [dma((4, 2, most))] * 2
        + [dma((2, 2, most))] * 2
        + [dma((n,))] * 2,
        compiler_params=pltpu.CompilerParams(collective_id=0, has_side_effects=True),
        name="gather_weights",
    )(*operands)
    return (
        full[0].reshape(-1, full[0].shape[-1]),
        full[1].reshape(-1, full[1].shape[-1]),
        full[2].reshape(-1, full[2].shape[-1]),
        full[3].reshape(-1, full[3].shape[-1]),
        full[4],
    )


def reduce_kernel(n, *refs):
    gq, go, gi, gb, gs, oq, oo, oi, ob, osm = refs[:10]
    (
        core_a,
        core_i,
        core_b,
        sent_b,
        chip_b,
        slot_a,
        slot_b,
        last_as,
        last_ar,
        last_bs,
        last_br,
        small_c,
        small_x,
        small_n,
        core_s,
        core_r,
        chip_s,
        chip_r,
        ring_s,
        ring_r,
        end_s,
        end_r,
        small_s,
        small_r,
    ) = refs[10:]
    me = Place(n)
    c, x = me.c, me.x
    half_q, half_o = gq.shape[2] // 2, go.shape[2] // 2
    quarter = gi.shape[2] // 4
    wide = half_q + half_o
    f32, bf16 = jnp.float32, jnp.bfloat16
    pending = []

    def go_remote(*args):
        copy = remote(*args)
        copy.start()
        pending.append(copy)

    me.greet()
    (more, less) = hops(n, 0)
    order = []
    for t in range(more):
        order.append(more - t)
        if t < less + 1 and less - t > 0:
            order.append(-(less - t))
    order.append(0)
    order_b = [-o for o in order]

    core = lambda k, src, dst, b: remote(src, dst, core_s.at[k, b], core_r.at[k, b], me.core_peer)
    for j, o in enumerate(order_b):
        b = me.at(o)
        go_remote(gi.at[b, :, cols(1 - c, 2 * quarter)], core_i.at[b], core_s.at[2, j], core_r.at[2, j], me.core_peer)
        go_remote(gb.at[b, pl.ds((1 - c) * 2, 2)], core_b.at[b], core_s.at[3, j], core_r.at[3, j], me.core_peer)
    go_remote(gs, small_c, small_s.at[0], small_r.at[0], me.core_peer)
    for j, o in enumerate(order):
        b = me.at(o)
        go_remote(gq.at[b, :, cols(1 - c, half_q)], core_a.at[b, :, pl.ds(0, half_q)], core_s.at[0, j], core_r.at[0, j], me.core_peer)
        go_remote(go.at[b, :, cols(1 - c, half_o)], core_a.at[b, :, pl.ds(half_q, half_o)], core_s.at[1, j], core_r.at[1, j], me.core_peer)

    def arrived(dst, send, recv):
        remote(dst, dst, send, recv, me.core_peer).wait_recv()

    for j, o in enumerate(order_b):
        b = me.at(o)
        arrived(core_i.at[b], core_s.at[2, j], core_r.at[2, j])
        arrived(core_b.at[b], core_s.at[3, j], core_r.at[3, j])
        sent_b[b, :, 0:quarter] = (
            gi[b, :, cols(c * 2 + 1 - x, quarter)].astype(f32)
            + core_i[b, :, cols(1 - x, quarter)].astype(f32)
        ).astype(bf16)
        sent_b[b, :, quarter : 2 * quarter] = (
            gb[b, c * 2 + 1 - x].astype(f32) + core_b[b, 1 - x].astype(f32)
        ).astype(bf16)
        go_remote(sent_b.at[b], chip_b.at[b], chip_s.at[j], chip_r.at[j], me.chip_peer)

    arrived(small_c, small_s.at[0], small_r.at[0])
    small_c[...] = small_c[...] + gs[...]
    go_remote(small_c, small_x, small_s.at[1], small_r.at[1], me.chip_peer)

    def ready_a(j):
        b = me.at(order[j])
        arrived(core_a.at[b, :, pl.ds(0, half_q)], core_s.at[0, j], core_r.at[0, j])
        arrived(core_a.at[b, :, pl.ds(half_q, half_o)], core_s.at[1, j], core_r.at[1, j])
        core_a[b, :, 0:half_q] = (
            core_a[b, :, 0:half_q].astype(f32) + gq[b, :, cols(c, half_q)].astype(f32)
        ).astype(bf16)
        core_a[b, :, half_q:wide] = (
            core_a[b, :, half_q:wide].astype(f32) + go[b, :, cols(c, half_o)].astype(f32)
        ).astype(bf16)

    def ready_b(j):
        b = me.at(order_b[j])
        arrived(chip_b.at[b], chip_s.at[j], chip_r.at[j])
        chip_b[b, :, 0:quarter] = (
            chip_b[b, :, 0:quarter].astype(f32)
            + (
                gi[b, :, cols(c * 2 + x, quarter)].astype(f32)
                + core_i[b, :, cols(x, quarter)].astype(f32)
            )
        ).astype(bf16)
        chip_b[b, :, quarter : 2 * quarter] = (
            chip_b[b, :, quarter : 2 * quarter].astype(f32)
            + (gb[b, c * 2 + x].astype(f32) + core_b[b, x].astype(f32))
        ).astype(bf16)

    def step(unit, way, t):
        total = core_a if unit == 0 else chip_b
        slots = slot_a if unit == 0 else slot_b
        offsets = order if unit == 0 else order_b
        count = hops(n, unit)[way]
        offset = (count - t) if way == 0 else -(count - t)
        (ready_a if unit == 0 else ready_b)(offsets.index(offset))
        b = me.at(offset)
        if t == 0:
            src = total.at[b]
        else:
            arrived(slots.at[way, t - 1], ring_s.at[unit, way, t - 1], ring_r.at[unit, way, t - 1])
            slots[way, t - 1] = (
                slots[way, t - 1].astype(f32) + total[b].astype(f32)
            ).astype(bf16)
            src = slots.at[way, t - 1]
        go_remote(
            src,
            slots.at[way, t],
            ring_s.at[unit, way, t],
            ring_r.at[unit, way, t],
            me.right if way == 0 else me.left,
        )

    def steps(unit, t):
        for way in range(2):
            if 0 <= t < hops(n, unit)[way]:
                step(unit, way, t)

    def small_spread():
        arrived(small_x, small_s.at[1], small_r.at[1])
        small_x[...] = small_x[...] + small_c[...]
        for j in range(1, n):
            other = (me.s + j) % n
            go_remote(small_x.at[other], small_n.at[me.s], small_s.at[1 + j], small_r.at[1 + j], (other, me.r))

    def finish(unit):
        total = core_a if unit == 0 else chip_b
        slots = slot_a if unit == 0 else slot_b
        (ready_a if unit == 0 else ready_b)(n - 1)
        acc = total[me.s].astype(f32)
        for way in range(2):
            last = hops(n, unit)[way] - 1
            arrived(slots.at[way, last], ring_s.at[unit, way, last], ring_r.at[unit, way, last])
            acc = acc + slots[way, last].astype(f32)
        (last_as if unit == 0 else last_bs)[...] = acc.astype(bf16)
        if unit == 0:
            go_remote(last_as, last_ar, end_s.at[0], end_r.at[0], me.chip_peer)
        else:
            go_remote(last_bs, last_br, end_s.at[1], end_r.at[1], me.chip_peer)

    for t in range(more + 1):
        steps(0, t)
        if t == 0:
            small_spread()
        if t == more:
            finish(0)
        steps(1, t - 1)
    finish(1)
    arrived(last_ar, end_s.at[0], end_r.at[0])
    both = last_as[...].astype(f32) + last_ar[...].astype(f32)
    oq[:, cols(c, half_q)] = both[:, 0:half_q]
    oo[:, cols(c, half_o)] = both[:, half_q:wide]
    for k, ref, width in ((2, oq, half_q), (3, oo, half_o)):
        place = ref.at[:, cols(c, width)]
        go_remote(place, place, end_s.at[k], end_r.at[k], me.core_peer)
    acc = last_bs[...].astype(f32)
    oi[:, cols(c * 2 + x, quarter)] = acc[:, 0:quarter]
    ob[c * 2 + x] = acc[:, quarter : 2 * quarter]
    small_n[me.s] = small_x[me.s]
    for j in range(1, n):
        arrived(small_n.at[(me.s + n - j) % n], small_s.at[1 + j], small_r.at[1 + j])
    acc = small_n[0]
    for j in range(1, n):
        acc = acc + small_n[j]
    osm[...] = acc
    arrived(last_br, end_s.at[1], end_r.at[1])
    acc = last_br[...].astype(f32)
    oi[:, cols(c * 2 + 1 - x, quarter)] = acc[:, 0:quarter]
    ob[c * 2 + 1 - x] = acc[:, quarter : 2 * quarter]
    place = oi.at[:, cols(c, 2 * quarter)]
    go_remote(place, place, end_s.at[4], end_r.at[4], me.core_peer)
    place = ob.at[pl.ds(c * 2, 2)]
    go_remote(place, place, end_s.at[5], end_r.at[5], me.core_peer)
    for k, ref, width in ((2, oq, half_q), (3, oo, half_o), (4, oi, 2 * quarter)):
        arrived(ref.at[:, cols(1 - c, width)], end_s.at[k], end_r.at[k])
    arrived(ob.at[pl.ds((1 - c) * 2, 2)], end_s.at[5], end_r.at[5])
    for copy in pending:
        copy.wait_send()


def reduce_gradients(n, d_qkv, d_out, d_in, d_back, small):
    rows = d_qkv.shape[0] // n
    bf16, f32 = jnp.bfloat16, jnp.float32
    operands = (
        d_qkv.reshape(n, rows, -1),
        d_out.reshape(n, rows, -1),
        d_in.reshape(n, rows, -1),
        d_back.reshape(n, 4, rows, -1),
        small,
    )
    quarter = d_in.shape[1] // 4
    wide = (d_qkv.shape[1] + d_out.shape[1]) // 2
    most = n // 2
    dma = pltpu.SemaphoreType.DMA
    vmem = pltpu.VMEM
    block = (rows, wide)
    outs = pl.pallas_call(
        functools.partial(reduce_kernel, n),
        out_shape=[jax.ShapeDtypeStruct(a.shape[1:], f32) for a in operands],
        in_specs=[pl.BlockSpec(memory_space=pltpu.VMEM)] * 5,
        out_specs=[pl.BlockSpec(memory_space=pltpu.VMEM)] * 5,
        scratch_shapes=[
            vmem((n,) + block, bf16),
            vmem((n, rows, 2 * quarter), bf16),
            vmem((n, 2, rows, quarter), bf16),
            vmem((n, rows, 2 * quarter), bf16),
            vmem((n, rows, 2 * quarter), bf16),
            vmem((2, most) + block, bf16),
            vmem((2, most, rows, 2 * quarter), bf16),
            vmem(block, bf16),
            vmem(block, bf16),
            vmem((rows, 2 * quarter), bf16),
            vmem((rows, 2 * quarter), bf16),
            vmem(small.shape, f32),
            vmem(small.shape, f32),
            vmem(small.shape, f32),
            dma((4, n)),
            dma((4, n)),
            dma((n,)),
            dma((n,)),
            dma((2, 2, most)),
            dma((2, 2, most)),
            dma((6,)),
            dma((6,)),
            dma((n + 1,)),
            dma((n + 1,)),
        ],
        compiler_params=pltpu.CompilerParams(
            collective_id=1, has_side_effects=True, vmem_limit_bytes=50 * 2**20
        ),
        name="reduce_gradients",
    )(*operands)
    outs = list(outs)
    outs[3] = outs[3].reshape(4 * rows, -1)
    return outs


def pack_small(parts, n):
    joined = jnp.concatenate([v.reshape(n, -1) for v in parts], 1)
    width = joined.shape[1]
    padded = -(-width // 2048) * 2048
    joined = jnp.pad(joined, ((0, 0), (0, padded - width)))
    return joined.reshape(n, padded // 128, 128)


def unpack_small(packed, sizes):
    flat = packed.reshape(packed.shape[0], -1)
    result, start = [], 0
    for size in sizes:
        result.append(flat[:, start : start + size].reshape(-1))
        start += size
    return result


def normalize(summed, gain_row, shift_row):
    average = jnp.mean(summed, -1, keepdims=True)
    centred = summed - average
    inv_scale = lax.rsqrt(jnp.mean(centred * centred, -1, keepdims=True) + EPSILON)
    unit_rows = centred * inv_scale
    return (
        unit_rows * gain_row.astype(jnp.float32) + shift_row.astype(jnp.float32),
        unit_rows,
        inv_scale,
    )


def norm_back(grad_unit, unit_rows, inv_scale):
    centred_grad = grad_unit - jnp.mean(grad_unit, -1, keepdims=True)
    return inv_scale * (
        centred_grad - unit_rows * jnp.mean(grad_unit * unit_rows, -1, keepdims=True)
    )


def gelu_exact(inputs):
    return jax.nn.gelu(inputs, approximate=False)


def body(
    n_shard,
    n_rep,
    tokens,
    labels,
    w_qkv,
    bias_qv,
    w_out,
    bias_out,
    w_in,
    bias_in,
    w_back,
    bias_back,
    gain_one,
    shift_one,
    gain_two,
    shift_two,
    cotangent,
):
    vectors = (
        bias_qv,
        bias_out,
        bias_in,
        bias_back,
        gain_one,
        shift_one,
        gain_two,
        shift_two,
    )
    sizes = [v.shape[0] for v in vectors]
    full_qkv, full_out, full_in, full_back, packed = gather_weights(
        n_shard, w_qkv, w_out, w_in, w_back, pack_small(vectors, 1)[0]
    )
    (
        full_bias_qv,
        full_bias_out,
        full_bias_in,
        full_bias_back,
        full_gain_one,
        full_shift_one,
        full_gain_two,
        full_shift_two,
    ) = unpack_small(packed, sizes)
    model_width = full_out.shape[0]
    row_count = tokens.shape[0]
    score_scale = 1.0 / math.sqrt(HEAD_DIM)
    qkv = jnp.dot(tokens, full_qkv, preferred_element_type=jnp.float32)
    bias_float = full_bias_qv.astype(jnp.float32)
    query_rows = (qkv[:, :model_width] + bias_float[:model_width]).astype(jnp.bfloat16)
    key_rows = qkv[:, model_width : 2 * model_width].astype(jnp.bfloat16)
    value_rows = (qkv[:, 2 * model_width :] + bias_float[model_width:]).astype(jnp.bfloat16)
    query_heads = query_rows.reshape(row_count, HEADS, HEAD_DIM)
    key_heads = key_rows.reshape(row_count, HEADS, HEAD_DIM)
    value_heads = value_rows.reshape(row_count, HEADS, HEAD_DIM)
    scores = (
        jnp.einsum("qhd,khd->hqk", query_heads, key_heads, preferred_element_type=jnp.float32)
        * score_scale
    )
    same_doc = labels[:, None] == labels[None, :]
    scores = jnp.where(same_doc[None], scores, -1000000000.0)
    highest = jnp.max(scores, -1, keepdims=True)
    exponent = jnp.exp(scores - highest)
    attention = exponent / jnp.sum(exponent, -1, keepdims=True)
    attention_low = attention.astype(jnp.bfloat16)
    mixed_heads = jnp.einsum(
        "hqk,khd->qhd", attention_low, value_heads, preferred_element_type=jnp.float32
    )
    mixed_heads = mixed_heads.reshape(row_count, model_width).astype(jnp.bfloat16)
    attn_out = jnp.dot(
        mixed_heads, full_out, preferred_element_type=jnp.float32
    ) + full_bias_out.astype(jnp.float32)
    first_out, unit_one, scale_one = normalize(
        tokens.astype(jnp.float32) + attn_out, full_gain_one, full_shift_one
    )
    first_low = first_out.astype(jnp.bfloat16)
    inner_sum = jnp.dot(
        first_low, full_in, preferred_element_type=jnp.float32
    ) + full_bias_in.astype(jnp.float32)
    activated = gelu_exact(inner_sum).astype(jnp.bfloat16)
    branch = jnp.dot(
        activated, full_back, preferred_element_type=jnp.float32
    ) + full_bias_back.astype(jnp.float32)
    final_out, unit_two, scale_two = normalize(first_out + branch, full_gain_two, full_shift_two)
    live_rows = (labels > 0).astype(jnp.float32)[:, None]
    output = (final_out * live_rows).astype(jnp.bfloat16)
    grad_final = cotangent.astype(jnp.float32) * live_rows
    d_gain_two = jnp.sum(grad_final * unit_two, 0)
    d_shift_two = jnp.sum(grad_final, 0)
    grad_mid = norm_back(grad_final * full_gain_two.astype(jnp.float32), unit_two, scale_two)
    grad_branch = grad_mid.astype(jnp.bfloat16)
    d_w_back = jnp.einsum("tf,td->fd", activated, grad_branch, preferred_element_type=jnp.float32)
    d_bias_back = jnp.sum(grad_branch.astype(jnp.float32), 0)
    grad_act = jnp.einsum(
        "td,fd->tf", grad_branch, full_back, preferred_element_type=jnp.float32
    )
    unused_value, gelu_pull = jax.vjp(gelu_exact, inner_sum)
    grad_inner = gelu_pull(grad_act)[0].astype(jnp.bfloat16)
    d_w_in = jnp.einsum("td,tf->df", first_low, grad_inner, preferred_element_type=jnp.float32)
    d_bias_in = jnp.sum(grad_inner.astype(jnp.float32), 0)
    grad_first = (
        jnp.einsum("tf,df->td", grad_inner, full_in, preferred_element_type=jnp.float32) + grad_mid
    )
    d_gain_one = jnp.sum(grad_first * unit_one, 0)
    d_shift_one = jnp.sum(grad_first, 0)
    grad_res = norm_back(grad_first * full_gain_one.astype(jnp.float32), unit_one, scale_one)
    grad_attn = grad_res.astype(jnp.bfloat16)
    d_w_out = jnp.einsum("td,te->de", mixed_heads, grad_attn, preferred_element_type=jnp.float32)
    d_bias_out = jnp.sum(grad_attn.astype(jnp.float32), 0)
    grad_mixed = jnp.einsum(
        "te,de->td", grad_attn, full_out, preferred_element_type=jnp.float32
    ).astype(jnp.bfloat16)
    grad_mixed_heads = grad_mixed.reshape(row_count, HEADS, HEAD_DIM)
    grad_attention = jnp.einsum(
        "qhd,khd->hqk", grad_mixed_heads, value_heads, preferred_element_type=jnp.float32
    )
    row_dot = jnp.sum(attention * grad_attention, -1, keepdims=True)
    grad_scores = (attention * (grad_attention - row_dot)).astype(jnp.bfloat16)
    grad_query = (
        jnp.einsum("hqk,khd->qhd", grad_scores, key_heads, preferred_element_type=jnp.float32)
        * score_scale
    ).astype(jnp.bfloat16)
    grad_keys = (
        jnp.einsum("hqk,qhd->khd", grad_scores, query_heads, preferred_element_type=jnp.float32)
        * score_scale
    ).astype(jnp.bfloat16)
    grad_values = jnp.einsum(
        "hqk,qhd->khd", attention_low, grad_mixed_heads, preferred_element_type=jnp.float32
    ).astype(jnp.bfloat16)
    grad_query = grad_query.reshape(row_count, model_width)
    grad_keys = grad_keys.reshape(row_count, model_width)
    grad_values = grad_values.reshape(row_count, model_width)
    grad_qkv = jnp.concatenate([grad_query, grad_keys, grad_values], 1)
    d_w_qkv = jnp.einsum("td,te->de", tokens, grad_qkv, preferred_element_type=jnp.float32)
    d_bias_qv = jnp.concatenate(
        [jnp.sum(grad_query.astype(jnp.float32), 0), jnp.sum(grad_values.astype(jnp.float32), 0)], 0
    )
    grad_tokens = (
        jnp.einsum("te,de->td", grad_qkv, full_qkv, preferred_element_type=jnp.float32) + grad_res
    )
    low_grads = [g.astype(jnp.bfloat16) for g in (d_w_qkv, d_w_out, d_w_in, d_w_back)]
    small_grads = pack_small(
        (
            d_bias_qv,
            d_bias_out,
            d_bias_in,
            d_bias_back,
            d_gain_one,
            d_shift_one,
            d_gain_two,
            d_shift_two,
        ),
        n_shard,
    )
    summed = reduce_gradients(n_shard, *low_grads, small_grads)
    if n_rep > QUAD:
        summed = [lax.psum(g, "rep") * (1.0 / QUAD) for g in summed]
    d_qkv, d_out, d_in, d_back, packed = summed
    vector = unpack_small(packed[None], sizes)
    return (
        output,
        grad_tokens,
        d_qkv,
        vector[0],
        d_out,
        vector[1],
        d_in,
        vector[2],
        d_back,
        vector[3],
        vector[4],
        vector[5],
        vector[6],
        vector[7],
    )


def solution(mesh):
    placed = (
        P(("shard", "rep"), None),
        P(("shard", "rep")),
        P("shard", None),
        P("shard"),
        P("shard", None),
        P("shard"),
        P("shard", None),
        P("shard"),
        P("shard", None),
        P("shard"),
        P("shard"),
        P("shard"),
        P("shard"),
        P("shard"),
        P(("shard", "rep"), None),
    )
    return jax.shard_map(
        functools.partial(body, mesh.shape["shard"], mesh.shape["rep"]),
        mesh=mesh,
        in_specs=placed,
        out_specs=(
            P(("shard", "rep"), None),
            P(("shard", "rep"), None),
            P("shard", None),
            P("shard"),
            P("shard", None),
            P("shard"),
            P("shard", None),
            P("shard"),
            P("shard", None),
            P("shard"),
            P("shard"),
            P("shard"),
            P("shard"),
            P("shard"),
        ),
        check_vma=False,
    )
```

```python
import functools
import math

import jax
import jax.numpy as jnp
from jax import lax
from jax.experimental import pallas as pl
from jax.experimental.pallas import tpu as pltpu
from jax.sharding import PartitionSpec as P

HEADS = 12
HEAD_DIM = 64
EPSILON = 1e-05
MESH = pl.DeviceIdType.MESH
QUAD = 4


class Place:
    def __init__(self, n_shard):
        self.n = n_shard
        self.half = n_shard // 2
        self.s = lax.axis_index("shard")
        self.r = lax.axis_index("rep")
        self.base = self.r - self.r % QUAD
        self.x = (self.r % QUAD) // 2
        self.c = self.r % 2
        z, y = self.s // 2, self.s % 2
        self.p = z * (1 - y) + (n_shard - 1 - z) * y
        self.core_peer = (self.s, self.base + self.x * 2 + (1 - self.c))
        self.chip_peer = (self.s, self.base + (1 - self.x) * 2 + self.c)
        self.right = (self.at(1), self.r)
        self.left = (self.at(-1), self.r)

    def at(self, offset):
        p = (self.p + offset + 2 * self.n) % self.n
        upper = p // self.half
        return (1 - upper) * 2 * p + upper * (2 * (self.n - 1 - p) + 1)

    def greet(self):
        barrier = pltpu.get_barrier_semaphore()
        targets = [((self.s + k) % self.n, self.r) for k in range(1, self.n)]
        targets += [self.core_peer, self.chip_peer]
        for device in targets:
            pl.semaphore_signal(barrier, inc=1, device_id=device, device_id_type=MESH)
        pl.semaphore_wait(barrier, len(targets))


def remote(src, dst, send, recv, device):
    return pltpu.make_async_remote_copy(
        src_ref=src,
        dst_ref=dst,
        send_sem=send,
        recv_sem=recv,
        device_id=device,
        device_id_type=MESH,
    )


def cols(index, width):
    return pl.ds(pl.multiple_of(index * width, 128), width)


def hops(n, unit):
    more, less = n // 2, n - 1 - n // 2
    return (more, less) if unit == 0 else (less, more)


def gather_kernel(n, *refs):
    ins, outs = refs[:5], refs[5:10]
    own_sem, ring_s, ring_r, chip_s, chip_r, core_s, core_r, far_s, far_r, small_s, small_r = refs[10:]
    me = Place(n)
    widths = (outs[0].shape[2] // 2, outs[1].shape[2] // 2, outs[2].shape[2] // 4)

    def part(k, block, x):
        if k < 2:
            return outs[k].at[block, :, cols(me.c, widths[k])]
        if k == 2:
            return outs[2].at[block, :, cols(me.c * 2 + x, widths[2])]
        return outs[3].at[block, me.c * 2 + x]

    def mine(k):
        if k < 2:
            return ins[k].at[:, cols(me.c, widths[k])]
        if k == 2:
            return ins[2].at[:, cols(me.c * 2 + me.x, widths[2])]
        return ins[3].at[me.c * 2 + me.x]

    me.greet()
    pending = []

    def ring(k, way, t):
        block = me.at(-t if way == 0 else t)
        src = mine(k) if t == 0 else part(k, block, me.x)
        copy = remote(
            src,
            part(k, block, me.x),
            ring_s.at[k, way, t],
            ring_r.at[k, way, t],
            me.right if way == 0 else me.left,
        )
        copy.start()
        pending.append(copy)

    def from_ring(k, way, t):
        block = me.at(-1 - t if way == 0 else 1 + t)
        here = part(k, block, me.x)
        remote(here, here, ring_s.at[k, way, t], ring_r.at[k, way, t], me.left).wait_recv()
        return block

    def to_peer(k, block, x, send, recv, device):
        copy = remote(part(k, block, x), part(k, block, x), send, recv, device)
        copy.start()
        pending.append(copy)

    order = (2, 3, 0, 1)
    for k in order:
        for way in range(2):
            ring(k, way, 0)
    for j in range(1, n):
        other = (me.s + j) % n
        copy = remote(ins[4], outs[4].at[me.s], small_s.at[j], small_r.at[j], (other, me.r))
        copy.start()
        pending.append(copy)
    own = [
        pltpu.make_async_copy(ins[k], outs[k].at[me.s], own_sem.at[k]) for k in range(5)
    ]
    for copy in own:
        copy.start()

    def from_chip(k, way, t):
        block = me.at(-1 - t if way == 0 else 1 + t)
        here = part(k, block, 1 - me.x)
        i = k - 2
        remote(here, here, chip_s.at[i, way, t], chip_r.at[i, way, t], me.chip_peer).wait_recv()
        to_peer(k, block, 1 - me.x, far_s.at[i, way, t], far_r.at[i, way, t], me.core_peer)

    most = n // 2
    for t in range(most + 1):
        for k in order:
            unit = 1 if k > 1 else 0
            for way in range(2):
                last = hops(n, unit)[way]
                if t < last:
                    block = from_ring(k, way, t)
                    if t + 1 < last:
                        ring(k, way, t + 1)
                    if unit:
                        to_peer(
                            k,
                            block,
                            me.x,
                            chip_s.at[k - 2, way, t],
                            chip_r.at[k - 2, way, t],
                            me.chip_peer,
                        )
                    to_peer(
                        k, block, me.x, core_s.at[k, way, t], core_r.at[k, way, t], me.core_peer
                    )
        for k in (2, 3):
            for way in range(2):
                if 0 <= t - 1 < hops(n, 1)[way]:
                    from_chip(k, way, t - 1)

    def peer_part(k, block, x):
        if k < 2:
            return outs[k].at[block, :, cols(1 - me.c, widths[k])]
        if k == 2:
            return outs[2].at[block, :, cols((1 - me.c) * 2 + x, widths[2])]
        return outs[3].at[block, (1 - me.c) * 2 + x]

    for k in range(4):
        unit = 1 if k > 1 else 0
        for way in range(2):
            for t in range(hops(n, unit)[way]):
                block = me.at(-1 - t if way == 0 else 1 + t)
                here = peer_part(k, block, me.x)
                remote(
                    here, here, core_s.at[k, way, t], core_r.at[k, way, t], me.core_peer
                ).wait_recv()
                if unit:
                    here = peer_part(k, block, 1 - me.x)
                    i = k - 2
                    remote(
                        here, here, far_s.at[i, way, t], far_r.at[i, way, t], me.core_peer
                    ).wait_recv()
    for j in range(1, n):
        here = outs[4].at[(me.s + n - j) % n]
        remote(here, here, small_s.at[j], small_r.at[j], me.core_peer).wait_recv()
    for copy in pending:
        copy.wait_send()
    for copy in own:
        copy.wait()


def gather_weights(n, w_qkv, w_out, w_in, w_back, small):
    rows = w_qkv.shape[0]
    w_back = w_back.reshape(4, rows, w_back.shape[1])
    operands = (w_qkv, w_out, w_in, w_back, small)
    most = n // 2
    dma = pltpu.SemaphoreType.DMA
    full = pl.pallas_call(
        functools.partial(gather_kernel, n),
        out_shape=[jax.ShapeDtypeStruct((n,) + a.shape, a.dtype) for a in operands],
        in_specs=[pl.BlockSpec(memory_space=pl.ANY)] * 5,
        out_specs=[pl.BlockSpec(memory_space=pl.ANY)] * 5,
        scratch_shapes=[dma((5,))]
        + [dma((4, 2, most))] * 2
        + [dma((2, 2, most))] * 2
        + [dma((4, 2, most))] * 2
        + [dma((2, 2, most))] * 2
        + [dma((n,))] * 2,
        compiler_params=pltpu.CompilerParams(collective_id=0, has_side_effects=True),
        name="gather_weights",
    )(*operands)
    return (
        full[0].reshape(-1, full[0].shape[-1]),
        full[1].reshape(-1, full[1].shape[-1]),
        full[2].reshape(-1, full[2].shape[-1]),
        full[3].reshape(-1, full[3].shape[-1]),
        full[4],
    )


def reduce_kernel(n, *refs):
    tok, mix, fst, act, gqkv, gattn, ginner, gbranch, gs, oq, oo, oi, ob, osm = refs[:14]
    (
        out_a,
        out_b,
        core_a,
        core_b,
        sent_b,
        chip_b,
        slot_a,
        slot_b,
        last_as,
        last_ar,
        last_bs,
        last_br,
        small_c,
        small_x,
        small_n,
        core_s,
        core_r,
        chip_s,
        chip_r,
        ring_s,
        ring_r,
        end_s,
        end_r,
        small_s,
        small_r,
    ) = refs[14:]
    me = Place(n)
    c, x = me.c, me.x
    half_q, half_o = gqkv.shape[1] // 2, gattn.shape[1] // 2
    quarter = ginner.shape[1] // 4
    wide = half_q + half_o
    f32, bf16 = jnp.float32, jnp.bfloat16
    pending = []

    def go_remote(*args):
        copy = remote(*args)
        copy.start()
        pending.append(copy)

    me.greet()
    (more, less) = hops(n, 0)
    order = []
    for t in range(more):
        order.append(more - t)
        if t < less + 1 and less - t > 0:
            order.append(-(less - t))
    order.append(0)
    order_b = [-o for o in order]

    def product(left, right):
        return jnp.dot(left, right, preferred_element_type=f32)

    def grad_a(b, core):
        return (
            product(tok[b], gqkv[:, cols(core, half_q)]),
            product(mix[b], gattn[:, cols(core, half_o)]),
        )

    def grad_b(b, q):
        return (
            product(fst[b], ginner[:, cols(q, quarter)]),
            product(act[b, q], gbranch[...]),
        )

    def send_b(j):
        b = me.at(order_b[j])
        for chip in range(2):
            first, second = grad_b(b, (1 - c) * 2 + chip)
            out_b[b, chip, :, 0:quarter] = first.astype(bf16)
            out_b[b, chip, :, quarter : 2 * quarter] = second.astype(bf16)
        go_remote(out_b.at[b], core_b.at[b], core_s.at[1, j], core_r.at[1, j], me.core_peer)

    def send_a(j):
        b = me.at(order[j])
        first, second = grad_a(b, 1 - c)
        out_a[b, :, 0:half_q] = first.astype(bf16)
        out_a[b, :, half_q:wide] = second.astype(bf16)
        go_remote(out_a.at[b], core_a.at[b], core_s.at[0, j], core_r.at[0, j], me.core_peer)

    def arrived(dst, send, recv):
        remote(dst, dst, send, recv, me.core_peer).wait_recv()

    def send_chip(j):
        b = me.at(order_b[j])
        arrived(core_b.at[b], core_s.at[1, j], core_r.at[1, j])
        first, second = grad_b(b, c * 2 + 1 - x)
        sent_b[b, :, 0:quarter] = (
            first + core_b[b, 1 - x, :, 0:quarter].astype(f32)
        ).astype(bf16)
        sent_b[b, :, quarter : 2 * quarter] = (
            second + core_b[b, 1 - x, :, quarter : 2 * quarter].astype(f32)
        ).astype(bf16)
        go_remote(sent_b.at[b], chip_b.at[b], chip_s.at[j], chip_r.at[j], me.chip_peer)

    ahead = 2
    for j in range(n + ahead):
        if j < n:
            send_b(j)
        if j == 0:
            go_remote(gs, small_c, small_s.at[0], small_r.at[0], me.core_peer)
        if j >= ahead:
            send_chip(j - ahead)
            send_a(j - ahead)

    arrived(small_c, small_s.at[0], small_r.at[0])
    small_c[...] = small_c[...] + gs[...]
    go_remote(small_c, small_x, small_s.at[1], small_r.at[1], me.chip_peer)

    def ready_a(j):
        b = me.at(order[j])
        arrived(core_a.at[b], core_s.at[0, j], core_r.at[0, j])
        first, second = grad_a(b, c)
        core_a[b, :, 0:half_q] = (core_a[b, :, 0:half_q].astype(f32) + first).astype(bf16)
        core_a[b, :, half_q:wide] = (core_a[b, :, half_q:wide].astype(f32) + second).astype(bf16)

    def ready_b(j):
        b = me.at(order_b[j])
        first, second = grad_b(b, c * 2 + x)
        first = first + core_b[b, x, :, 0:quarter].astype(f32)
        second = second + core_b[b, x, :, quarter : 2 * quarter].astype(f32)
        arrived(chip_b.at[b], chip_s.at[j], chip_r.at[j])
        chip_b[b, :, 0:quarter] = (chip_b[b, :, 0:quarter].astype(f32) + first).astype(bf16)
        chip_b[b, :, quarter : 2 * quarter] = (
            chip_b[b, :, quarter : 2 * quarter].astype(f32) + second
        ).astype(bf16)

    def step(unit, way, t):
        total = core_a if unit == 0 else chip_b
        slots = slot_a if unit == 0 else slot_b
        offsets = order if unit == 0 else order_b
        count = hops(n, unit)[way]
        offset = (count - t) if way == 0 else -(count - t)
        (ready_a if unit == 0 else ready_b)(offsets.index(offset))
        b = me.at(offset)
        if t == 0:
            src = total.at[b]
        else:
            arrived(slots.at[way, t - 1], ring_s.at[unit, way, t - 1], ring_r.at[unit, way, t - 1])
            slots[way, t - 1] = (
                slots[way, t - 1].astype(f32) + total[b].astype(f32)
            ).astype(bf16)
            src = slots.at[way, t - 1]
        go_remote(
            src,
            slots.at[way, t],
            ring_s.at[unit, way, t],
            ring_r.at[unit, way, t],
            me.right if way == 0 else me.left,
        )

    def steps(unit, t):
        for way in range(2):
            if 0 <= t < hops(n, unit)[way]:
                step(unit, way, t)

    def small_spread():
        arrived(small_x, small_s.at[1], small_r.at[1])
        small_x[...] = small_x[...] + small_c[...]
        for j in range(1, n):
            other = (me.s + j) % n
            go_remote(small_x.at[other], small_n.at[me.s], small_s.at[1 + j], small_r.at[1 + j], (other, me.r))

    def finish(unit):
        total = core_a if unit == 0 else chip_b
        slots = slot_a if unit == 0 else slot_b
        (ready_a if unit == 0 else ready_b)(n - 1)
        acc = total[me.s].astype(f32)
        for way in range(2):
            last = hops(n, unit)[way] - 1
            arrived(slots.at[way, last], ring_s.at[unit, way, last], ring_r.at[unit, way, last])
            acc = acc + slots[way, last].astype(f32)
        (last_as if unit == 0 else last_bs)[...] = acc.astype(bf16)
        if unit == 0:
            go_remote(last_as, last_ar, end_s.at[0], end_r.at[0], me.chip_peer)
        else:
            go_remote(last_bs, last_br, end_s.at[1], end_r.at[1], me.chip_peer)

    for t in range(more + 1):
        steps(0, t)
        if t == 0:
            small_spread()
        if t == more:
            finish(0)
        steps(1, t - 1)
    finish(1)
    arrived(last_ar, end_s.at[0], end_r.at[0])
    both = last_as[...].astype(f32) + last_ar[...].astype(f32)
    oq[:, cols(c, half_q)] = both[:, 0:half_q]
    oo[:, cols(c, half_o)] = both[:, half_q:wide]
    for k, ref, width in ((2, oq, half_q), (3, oo, half_o)):
        place = ref.at[:, cols(c, width)]
        go_remote(place, place, end_s.at[k], end_r.at[k], me.core_peer)
    acc = last_bs[...].astype(f32)
    oi[:, cols(c * 2 + x, quarter)] = acc[:, 0:quarter]
    ob[c * 2 + x] = acc[:, quarter : 2 * quarter]
    small_n[me.s] = small_x[me.s]
    for j in range(1, n):
        arrived(small_n.at[(me.s + n - j) % n], small_s.at[1 + j], small_r.at[1 + j])
    acc = small_n[0]
    for j in range(1, n):
        acc = acc + small_n[j]
    osm[...] = acc
    arrived(last_br, end_s.at[1], end_r.at[1])
    acc = last_br[...].astype(f32)
    oi[:, cols(c * 2 + 1 - x, quarter)] = acc[:, 0:quarter]
    ob[c * 2 + 1 - x] = acc[:, quarter : 2 * quarter]
    place = oi.at[:, cols(c, 2 * quarter)]
    go_remote(place, place, end_s.at[4], end_r.at[4], me.core_peer)
    place = ob.at[pl.ds(c * 2, 2)]
    go_remote(place, place, end_s.at[5], end_r.at[5], me.core_peer)
    for k, ref, width in ((2, oq, half_q), (3, oo, half_o), (4, oi, 2 * quarter)):
        arrived(ref.at[:, cols(1 - c, width)], end_s.at[k], end_r.at[k])
    arrived(ob.at[pl.ds((1 - c) * 2, 2)], end_s.at[5], end_r.at[5])
    for copy in pending:
        copy.wait_send()


def reduce_gradients(n, pairs, small):
    f32, bf16 = jnp.float32, jnp.bfloat16
    tokens = pairs[0][0].shape[0]
    turned = [left.T for left, _ in pairs]
    rows = turned[0].shape[0] // n
    turned = [a.reshape(n, rows, tokens) for a in turned[:3]] + [
        turned[3].reshape(n, 4, rows, tokens)
    ]
    grads = [right for _, right in pairs]
    operands = (*turned, *grads, small)
    quarter = grads[2].shape[1] // 4
    wide = (grads[0].shape[1] + grads[1].shape[1]) // 2
    shapes = [(rows, g.shape[1]) for g in grads[:3]] + [(4, rows, grads[3].shape[1]), small.shape[1:]]
    most = n // 2
    dma = pltpu.SemaphoreType.DMA
    vmem = pltpu.VMEM
    block = (rows, wide)
    outs = pl.pallas_call(
        functools.partial(reduce_kernel, n),
        out_shape=[jax.ShapeDtypeStruct(shape, f32) for shape in shapes],
        in_specs=[pl.BlockSpec(memory_space=pltpu.VMEM)] * 9,
        out_specs=[pl.BlockSpec(memory_space=pltpu.VMEM)] * 5,
        scratch_shapes=[
            vmem((n,) + block, bf16),
            vmem((n, 2, rows, 2 * quarter), bf16),
            vmem((n,) + block, bf16),
            vmem((n, 2, rows, 2 * quarter), bf16),
            vmem((n, rows, 2 * quarter), bf16),
            vmem((n, rows, 2 * quarter), bf16),
            vmem((2, most) + block, bf16),
            vmem((2, most, rows, 2 * quarter), bf16),
            vmem(block, bf16),
            vmem(block, bf16),
            vmem((rows, 2 * quarter), bf16),
            vmem((rows, 2 * quarter), bf16),
            vmem(small.shape, f32),
            vmem(small.shape, f32),
            vmem(small.shape, f32),
            dma((2, n)),
            dma((2, n)),
            dma((n,)),
            dma((n,)),
            dma((2, 2, most)),
            dma((2, 2, most)),
            dma((6,)),
            dma((6,)),
            dma((n + 1,)),
            dma((n + 1,)),
        ],
        compiler_params=pltpu.CompilerParams(
            collective_id=1, has_side_effects=True, vmem_limit_bytes=50 * 2**20
        ),
        name="reduce_gradients",
    )(*operands)
    outs = list(outs)
    outs[3] = outs[3].reshape(4 * rows, -1)
    return outs


def pack_small(parts, n):
    joined = jnp.concatenate([v.reshape(n, -1) for v in parts], 1)
    width = joined.shape[1]
    padded = -(-width // 2048) * 2048
    joined = jnp.pad(joined, ((0, 0), (0, padded - width)))
    return joined.reshape(n, padded // 128, 128)


def unpack_small(packed, sizes):
    flat = packed.reshape(packed.shape[0], -1)
    result, start = [], 0
    for size in sizes:
        result.append(flat[:, start : start + size].reshape(-1))
        start += size
    return result


def normalize(summed, gain_row, shift_row):
    average = jnp.mean(summed, -1, keepdims=True)
    centred = summed - average
    inv_scale = lax.rsqrt(jnp.mean(centred * centred, -1, keepdims=True) + EPSILON)
    unit_rows = centred * inv_scale
    return (
        unit_rows * gain_row.astype(jnp.float32) + shift_row.astype(jnp.float32),
        unit_rows,
        inv_scale,
    )


def norm_back(grad_unit, unit_rows, inv_scale):
    centred_grad = grad_unit - jnp.mean(grad_unit, -1, keepdims=True)
    return inv_scale * (
        centred_grad - unit_rows * jnp.mean(grad_unit * unit_rows, -1, keepdims=True)
    )


def gelu_exact(inputs):
    return jax.nn.gelu(inputs, approximate=False)


def body(
    n_shard,
    n_rep,
    tokens,
    labels,
    w_qkv,
    bias_qv,
    w_out,
    bias_out,
    w_in,
    bias_in,
    w_back,
    bias_back,
    gain_one,
    shift_one,
    gain_two,
    shift_two,
    cotangent,
):
    vectors = (
        bias_qv,
        bias_out,
        bias_in,
        bias_back,
        gain_one,
        shift_one,
        gain_two,
        shift_two,
    )
    sizes = [v.shape[0] for v in vectors]
    full_qkv, full_out, full_in, full_back, packed = gather_weights(
        n_shard, w_qkv, w_out, w_in, w_back, pack_small(vectors, 1)[0]
    )
    (
        full_bias_qv,
        full_bias_out,
        full_bias_in,
        full_bias_back,
        full_gain_one,
        full_shift_one,
        full_gain_two,
        full_shift_two,
    ) = unpack_small(packed, sizes)
    model_width = full_out.shape[0]
    row_count = tokens.shape[0]
    score_scale = 1.0 / math.sqrt(HEAD_DIM)
    qkv = jnp.dot(tokens, full_qkv, preferred_element_type=jnp.float32)
    bias_float = full_bias_qv.astype(jnp.float32)
    query_rows = (qkv[:, :model_width] + bias_float[:model_width]).astype(jnp.bfloat16)
    key_rows = qkv[:, model_width : 2 * model_width].astype(jnp.bfloat16)
    value_rows = (qkv[:, 2 * model_width :] + bias_float[model_width:]).astype(jnp.bfloat16)
    query_heads = query_rows.reshape(row_count, HEADS, HEAD_DIM)
    key_heads = key_rows.reshape(row_count, HEADS, HEAD_DIM)
    value_heads = value_rows.reshape(row_count, HEADS, HEAD_DIM)
    scores = (
        jnp.einsum("qhd,khd->hqk", query_heads, key_heads, preferred_element_type=jnp.float32)
        * score_scale
    )
    same_doc = labels[:, None] == labels[None, :]
    scores = jnp.where(same_doc[None], scores, -1000000000.0)
    highest = jnp.max(scores, -1, keepdims=True)
    exponent = jnp.exp(scores - highest)
    attention = exponent / jnp.sum(exponent, -1, keepdims=True)
    attention_low = attention.astype(jnp.bfloat16)
    mixed_heads = jnp.einsum(
        "hqk,khd->qhd", attention_low, value_heads, preferred_element_type=jnp.float32
    )
    mixed_heads = mixed_heads.reshape(row_count, model_width).astype(jnp.bfloat16)
    attn_out = jnp.dot(
        mixed_heads, full_out, preferred_element_type=jnp.float32
    ) + full_bias_out.astype(jnp.float32)
    first_out, unit_one, scale_one = normalize(
        tokens.astype(jnp.float32) + attn_out, full_gain_one, full_shift_one
    )
    first_low = first_out.astype(jnp.bfloat16)
    inner_sum = jnp.dot(
        first_low, full_in, preferred_element_type=jnp.float32
    ) + full_bias_in.astype(jnp.float32)
    activated = gelu_exact(inner_sum).astype(jnp.bfloat16)
    branch = jnp.dot(
        activated, full_back, preferred_element_type=jnp.float32
    ) + full_bias_back.astype(jnp.float32)
    final_out, unit_two, scale_two = normalize(first_out + branch, full_gain_two, full_shift_two)
    live_rows = (labels > 0).astype(jnp.float32)[:, None]
    output = (final_out * live_rows).astype(jnp.bfloat16)
    grad_final = cotangent.astype(jnp.float32) * live_rows
    d_gain_two = jnp.sum(grad_final * unit_two, 0)
    d_shift_two = jnp.sum(grad_final, 0)
    grad_mid = norm_back(grad_final * full_gain_two.astype(jnp.float32), unit_two, scale_two)
    grad_branch = grad_mid.astype(jnp.bfloat16)
    d_bias_back = jnp.sum(grad_branch.astype(jnp.float32), 0)
    grad_act = jnp.einsum(
        "td,fd->tf", grad_branch, full_back, preferred_element_type=jnp.float32
    )
    unused_value, gelu_pull = jax.vjp(gelu_exact, inner_sum)
    grad_inner = gelu_pull(grad_act)[0].astype(jnp.bfloat16)
    d_bias_in = jnp.sum(grad_inner.astype(jnp.float32), 0)
    grad_first = (
        jnp.einsum("tf,df->td", grad_inner, full_in, preferred_element_type=jnp.float32) + grad_mid
    )
    d_gain_one = jnp.sum(grad_first * unit_one, 0)
    d_shift_one = jnp.sum(grad_first, 0)
    grad_res = norm_back(grad_first * full_gain_one.astype(jnp.float32), unit_one, scale_one)
    grad_attn = grad_res.astype(jnp.bfloat16)
    d_bias_out = jnp.sum(grad_attn.astype(jnp.float32), 0)
    grad_mixed = jnp.einsum(
        "te,de->td", grad_attn, full_out, preferred_element_type=jnp.float32
    ).astype(jnp.bfloat16)
    grad_mixed_heads = grad_mixed.reshape(row_count, HEADS, HEAD_DIM)
    grad_attention = jnp.einsum(
        "qhd,khd->hqk", grad_mixed_heads, value_heads, preferred_element_type=jnp.float32
    )
    row_dot = jnp.sum(attention * grad_attention, -1, keepdims=True)
    grad_scores = (attention * (grad_attention - row_dot)).astype(jnp.bfloat16)
    grad_query = (
        jnp.einsum("hqk,khd->qhd", grad_scores, key_heads, preferred_element_type=jnp.float32)
        * score_scale
    ).astype(jnp.bfloat16)
    grad_keys = (
        jnp.einsum("hqk,qhd->khd", grad_scores, query_heads, preferred_element_type=jnp.float32)
        * score_scale
    ).astype(jnp.bfloat16)
    grad_values = jnp.einsum(
        "hqk,qhd->khd", attention_low, grad_mixed_heads, preferred_element_type=jnp.float32
    ).astype(jnp.bfloat16)
    grad_query = grad_query.reshape(row_count, model_width)
    grad_keys = grad_keys.reshape(row_count, model_width)
    grad_values = grad_values.reshape(row_count, model_width)
    grad_qkv = jnp.concatenate([grad_query, grad_keys, grad_values], 1)
    d_bias_qv = jnp.concatenate(
        [jnp.sum(grad_query.astype(jnp.float32), 0), jnp.sum(grad_values.astype(jnp.float32), 0)], 0
    )
    grad_tokens = (
        jnp.einsum("te,de->td", grad_qkv, full_qkv, preferred_element_type=jnp.float32) + grad_res
    )
    pairs = (
        (tokens, grad_qkv),
        (mixed_heads, grad_attn),
        (first_low, grad_inner),
        (activated, grad_branch),
    )
    small_grads = pack_small(
        (
            d_bias_qv,
            d_bias_out,
            d_bias_in,
            d_bias_back,
            d_gain_one,
            d_shift_one,
            d_gain_two,
            d_shift_two,
        ),
        n_shard,
    )
    summed = reduce_gradients(n_shard, pairs, small_grads)
    if n_rep > QUAD:
        summed = [lax.psum(g, "rep") * (1.0 / QUAD) for g in summed]
    d_qkv, d_out, d_in, d_back, packed = summed
    vector = unpack_small(packed[None], sizes)
    return (
        output,
        grad_tokens,
        d_qkv,
        vector[0],
        d_out,
        vector[1],
        d_in,
        vector[2],
        d_back,
        vector[3],
        vector[4],
        vector[5],
        vector[6],
        vector[7],
    )


def solution(mesh):
    placed = (
        P(("shard", "rep"), None),
        P(("shard", "rep")),
        P("shard", None),
        P("shard"),
        P("shard", None),
        P("shard"),
        P("shard", None),
        P("shard"),
        P("shard", None),
        P("shard"),
        P("shard"),
        P("shard"),
        P("shard"),
        P("shard"),
        P(("shard", "rep"), None),
    )
    return jax.shard_map(
        functools.partial(body, mesh.shape["shard"], mesh.shape["rep"]),
        mesh=mesh,
        in_specs=placed,
        out_specs=(
            P(("shard", "rep"), None),
            P(("shard", "rep"), None),
            P("shard", None),
            P("shard"),
            P("shard", None),
            P("shard"),
            P("shard", None),
            P("shard"),
            P("shard", None),
            P("shard"),
            P("shard"),
            P("shard"),
            P("shard"),
            P("shard"),
        ),
        check_vma=False,
    )
```

```python
import functools
import math

import jax
import jax.numpy as jnp
from jax import lax
from jax.experimental import pallas as pl
from jax.experimental.pallas import tpu as pltpu
from jax.sharding import PartitionSpec as P

HEADS = 12
HEAD_DIM = 64
EPSILON = 1e-05
MESH = pl.DeviceIdType.MESH
QUAD = 4


class Place:
    def __init__(self, n_shard):
        self.n = n_shard
        self.half = n_shard // 2
        self.s = lax.axis_index("shard")
        self.r = lax.axis_index("rep")
        self.base = self.r - self.r % QUAD
        self.x = (self.r % QUAD) // 2
        self.c = self.r % 2
        z, y = self.s // 2, self.s % 2
        self.p = z * (1 - y) + (n_shard - 1 - z) * y
        self.core_peer = (self.s, self.base + self.x * 2 + (1 - self.c))
        self.chip_peer = (self.s, self.base + (1 - self.x) * 2 + self.c)
        self.right = (self.at(1), self.r)
        self.left = (self.at(-1), self.r)

    def at(self, offset):
        p = (self.p + offset + 2 * self.n) % self.n
        upper = p // self.half
        return (1 - upper) * 2 * p + upper * (2 * (self.n - 1 - p) + 1)

    def greet(self):
        barrier = pltpu.get_barrier_semaphore()
        targets = [((self.s + k) % self.n, self.r) for k in range(1, self.n)]
        targets += [self.core_peer, self.chip_peer]
        for device in targets:
            pl.semaphore_signal(barrier, inc=1, device_id=device, device_id_type=MESH)
        pl.semaphore_wait(barrier, len(targets))


def remote(src, dst, send, recv, device):
    return pltpu.make_async_remote_copy(
        src_ref=src,
        dst_ref=dst,
        send_sem=send,
        recv_sem=recv,
        device_id=device,
        device_id_type=MESH,
    )


def cols(index, width):
    return pl.ds(pl.multiple_of(index * width, 128), width)


def hops(n, unit):
    more, less = n // 2, n - 1 - n // 2
    return (more, less) if unit == 0 else (less, more)


def gather_kernel(n, *refs):
    ins, outs = refs[:5], refs[5:10]
    own_sem, ring_s, ring_r, chip_s, chip_r, core_s, core_r, far_s, far_r, small_s, small_r = refs[10:]
    me = Place(n)
    widths = (outs[0].shape[2] // 2, outs[1].shape[2] // 2, outs[2].shape[2] // 4)

    def part(k, block, x):
        if k < 2:
            return outs[k].at[block, :, cols(me.c, widths[k])]
        if k == 2:
            return outs[2].at[block, :, cols(me.c * 2 + x, widths[2])]
        return outs[3].at[block, me.c * 2 + x]

    def mine(k):
        if k < 2:
            return ins[k].at[:, cols(me.c, widths[k])]
        if k == 2:
            return ins[2].at[:, cols(me.c * 2 + me.x, widths[2])]
        return ins[3].at[me.c * 2 + me.x]

    me.greet()
    pending = []

    def ring(k, way, t):
        block = me.at(-t if way == 0 else t)
        src = mine(k) if t == 0 else part(k, block, me.x)
        copy = remote(
            src,
            part(k, block, me.x),
            ring_s.at[k, way, t],
            ring_r.at[k, way, t],
            me.right if way == 0 else me.left,
        )
        copy.start()
        pending.append(copy)

    def from_ring(k, way, t):
        block = me.at(-1 - t if way == 0 else 1 + t)
        here = part(k, block, me.x)
        remote(here, here, ring_s.at[k, way, t], ring_r.at[k, way, t], me.left).wait_recv()
        return block

    def to_peer(k, block, x, send, recv, device):
        copy = remote(part(k, block, x), part(k, block, x), send, recv, device)
        copy.start()
        pending.append(copy)

    order = (2, 3, 0, 1)
    for k in order:
        for way in range(2):
            ring(k, way, 0)
    for j in range(1, n):
        other = (me.s + j) % n
        copy = remote(ins[4], outs[4].at[me.s], small_s.at[j], small_r.at[j], (other, me.r))
        copy.start()
        pending.append(copy)
    own = [
        pltpu.make_async_copy(ins[k], outs[k].at[me.s], own_sem.at[k]) for k in range(5)
    ]
    for copy in own:
        copy.start()

    def from_chip(k, way, t):
        block = me.at(-1 - t if way == 0 else 1 + t)
        here = part(k, block, 1 - me.x)
        i = k - 2
        remote(here, here, chip_s.at[i, way, t], chip_r.at[i, way, t], me.chip_peer).wait_recv()
        to_peer(k, block, 1 - me.x, far_s.at[i, way, t], far_r.at[i, way, t], me.core_peer)

    most = n // 2
    for t in range(most + 1):
        for k in order:
            unit = 1 if k > 1 else 0
            for way in range(2):
                last = hops(n, unit)[way]
                if t < last:
                    block = from_ring(k, way, t)
                    if t + 1 < last:
                        ring(k, way, t + 1)
                    if unit:
                        to_peer(
                            k,
                            block,
                            me.x,
                            chip_s.at[k - 2, way, t],
                            chip_r.at[k - 2, way, t],
                            me.chip_peer,
                        )
                    to_peer(
                        k, block, me.x, core_s.at[k, way, t], core_r.at[k, way, t], me.core_peer
                    )
        for k in (2, 3):
            for way in range(2):
                if 0 <= t - 1 < hops(n, 1)[way]:
                    from_chip(k, way, t - 1)

    def peer_part(k, block, x):
        if k < 2:
            return outs[k].at[block, :, cols(1 - me.c, widths[k])]
        if k == 2:
            return outs[2].at[block, :, cols((1 - me.c) * 2 + x, widths[2])]
        return outs[3].at[block, (1 - me.c) * 2 + x]

    for k in range(4):
        unit = 1 if k > 1 else 0
        for way in range(2):
            for t in range(hops(n, unit)[way]):
                block = me.at(-1 - t if way == 0 else 1 + t)
                here = peer_part(k, block, me.x)
                remote(
                    here, here, core_s.at[k, way, t], core_r.at[k, way, t], me.core_peer
                ).wait_recv()
                if unit:
                    here = peer_part(k, block, 1 - me.x)
                    i = k - 2
                    remote(
                        here, here, far_s.at[i, way, t], far_r.at[i, way, t], me.core_peer
                    ).wait_recv()
    for j in range(1, n):
        here = outs[4].at[(me.s + n - j) % n]
        remote(here, here, small_s.at[j], small_r.at[j], me.core_peer).wait_recv()
    for copy in pending:
        copy.wait_send()
    for copy in own:
        copy.wait()


def gather_weights(n, w_qkv, w_out, w_in, w_back, small):
    rows = w_qkv.shape[0]
    w_back = w_back.reshape(4, rows, w_back.shape[1])
    operands = (w_qkv, w_out, w_in, w_back, small)
    most = n // 2
    dma = pltpu.SemaphoreType.DMA
    full = pl.pallas_call(
        functools.partial(gather_kernel, n),
        out_shape=[jax.ShapeDtypeStruct((n,) + a.shape, a.dtype) for a in operands],
        in_specs=[pl.BlockSpec(memory_space=pl.ANY)] * 5,
        out_specs=[pl.BlockSpec(memory_space=pl.ANY)] * 5,
        scratch_shapes=[dma((5,))]
        + [dma((4, 2, most))] * 2
        + [dma((2, 2, most))] * 2
        + [dma((4, 2, most))] * 2
        + [dma((2, 2, most))] * 2
        + [dma((n,))] * 2,
        compiler_params=pltpu.CompilerParams(collective_id=0, has_side_effects=True),
        name="gather_weights",
    )(*operands)
    return (
        full[0].reshape(-1, full[0].shape[-1]),
        full[1].reshape(-1, full[1].shape[-1]),
        full[2].reshape(-1, full[2].shape[-1]),
        full[3].reshape(-1, full[3].shape[-1]),
        full[4],
    )


def reduce_kernel(n, *refs):
    tok, mix, fst, act, gqkv, gattn, ginner, gbranch, gs, oq, oo, oi, ob, osm = refs[:14]
    (
        out_a,
        out_b,
        core_a,
        core_b,
        sent_b,
        chip_b,
        slot_a,
        slot_b,
        last_as,
        last_ar,
        last_bs,
        last_br,
        small_c,
        small_x,
        small_n,
        core_s,
        core_r,
        chip_s,
        chip_r,
        ring_s,
        ring_r,
        end_s,
        end_r,
        small_s,
        small_r,
    ) = refs[14:]
    me = Place(n)
    c, x = me.c, me.x
    half_q, half_o = gqkv.shape[1] // 2, gattn.shape[1] // 2
    quarter = ginner.shape[1] // 4
    wide = half_q + half_o
    f32, bf16 = jnp.float32, jnp.bfloat16
    pending = []

    def go_remote(*args):
        copy = remote(*args)
        copy.start()
        pending.append(copy)

    me.greet()
    (more, less) = hops(n, 0)
    order = []
    for t in range(more):
        order.append(more - t)
        if t < less + 1 and less - t > 0:
            order.append(-(less - t))
    order.append(0)
    order_b = [-o for o in order]

    def product(left, right):
        return jnp.dot(left, right, preferred_element_type=f32)

    def grad_a(b, core):
        return (
            product(tok[b], gqkv[:, cols(core, half_q)]),
            product(mix[b], gattn[:, cols(core, half_o)]),
        )

    def grad_b(b, q):
        return (
            product(fst[b], ginner[:, cols(q, quarter)]),
            product(act[b, q], gbranch[...]),
        )

    def send_b(j):
        b = me.at(order_b[j])
        for chip in range(2):
            first, second = grad_b(b, (1 - c) * 2 + chip)
            out_b[b, chip, :, 0:quarter] = first.astype(bf16)
            out_b[b, chip, :, quarter : 2 * quarter] = second.astype(bf16)
        go_remote(out_b.at[b], core_b.at[b], core_s.at[1, j], core_r.at[1, j], me.core_peer)

    def send_a(j):
        b = me.at(order[j])
        first, second = grad_a(b, 1 - c)
        out_a[b, :, 0:half_q] = first.astype(bf16)
        out_a[b, :, half_q:wide] = second.astype(bf16)
        go_remote(out_a.at[b], core_a.at[b], core_s.at[0, j], core_r.at[0, j], me.core_peer)

    def arrived(dst, send, recv):
        remote(dst, dst, send, recv, me.core_peer).wait_recv()

    def send_chip(j):
        b = me.at(order_b[j])
        arrived(core_b.at[b], core_s.at[1, j], core_r.at[1, j])
        first, second = grad_b(b, c * 2 + 1 - x)
        sent_b[b, :, 0:quarter] = (
            first + core_b[b, 1 - x, :, 0:quarter].astype(f32)
        ).astype(bf16)
        sent_b[b, :, quarter : 2 * quarter] = (
            second + core_b[b, 1 - x, :, quarter : 2 * quarter].astype(f32)
        ).astype(bf16)
        go_remote(sent_b.at[b], chip_b.at[b], chip_s.at[j], chip_r.at[j], me.chip_peer)

    ahead = 2
    for j in range(n + ahead):
        if j < n:
            send_b(j)
        if j == 0:
            go_remote(gs, small_c, small_s.at[0], small_r.at[0], me.core_peer)
        if j >= ahead:
            send_chip(j - ahead)
            send_a(j - ahead)

    arrived(small_c, small_s.at[0], small_r.at[0])
    small_c[...] = small_c[...] + gs[...]
    go_remote(small_c, small_x, small_s.at[1], small_r.at[1], me.chip_peer)

    def ready_a(j):
        b = me.at(order[j])
        arrived(core_a.at[b], core_s.at[0, j], core_r.at[0, j])
        first, second = grad_a(b, c)
        core_a[b, :, 0:half_q] = (core_a[b, :, 0:half_q].astype(f32) + first).astype(bf16)
        core_a[b, :, half_q:wide] = (core_a[b, :, half_q:wide].astype(f32) + second).astype(bf16)

    def ready_b(j):
        b = me.at(order_b[j])
        first, second = grad_b(b, c * 2 + x)
        first = first + core_b[b, x, :, 0:quarter].astype(f32)
        second = second + core_b[b, x, :, quarter : 2 * quarter].astype(f32)
        arrived(chip_b.at[b], chip_s.at[j], chip_r.at[j])
        chip_b[b, :, 0:quarter] = (chip_b[b, :, 0:quarter].astype(f32) + first).astype(bf16)
        chip_b[b, :, quarter : 2 * quarter] = (
            chip_b[b, :, quarter : 2 * quarter].astype(f32) + second
        ).astype(bf16)

    def step(unit, way, t):
        total = core_a if unit == 0 else chip_b
        slots = slot_a if unit == 0 else slot_b
        offsets = order if unit == 0 else order_b
        count = hops(n, unit)[way]
        offset = (count - t) if way == 0 else -(count - t)
        (ready_a if unit == 0 else ready_b)(offsets.index(offset))
        b = me.at(offset)
        if t == 0:
            src = total.at[b]
        else:
            arrived(slots.at[way, t - 1], ring_s.at[unit, way, t - 1], ring_r.at[unit, way, t - 1])
            slots[way, t - 1] = (
                slots[way, t - 1].astype(f32) + total[b].astype(f32)
            ).astype(bf16)
            src = slots.at[way, t - 1]
        go_remote(
            src,
            slots.at[way, t],
            ring_s.at[unit, way, t],
            ring_r.at[unit, way, t],
            me.right if way == 0 else me.left,
        )

    def steps(unit, t):
        for way in range(2):
            if 0 <= t < hops(n, unit)[way]:
                step(unit, way, t)

    def small_spread():
        arrived(small_x, small_s.at[1], small_r.at[1])
        small_x[...] = small_x[...] + small_c[...]
        for j in range(1, n):
            other = (me.s + j) % n
            go_remote(small_x.at[other], small_n.at[me.s], small_s.at[1 + j], small_r.at[1 + j], (other, me.r))

    def finish(unit):
        total = core_a if unit == 0 else chip_b
        slots = slot_a if unit == 0 else slot_b
        (ready_a if unit == 0 else ready_b)(n - 1)
        acc = total[me.s].astype(f32)
        for way in range(2):
            last = hops(n, unit)[way] - 1
            arrived(slots.at[way, last], ring_s.at[unit, way, last], ring_r.at[unit, way, last])
            acc = acc + slots[way, last].astype(f32)
        (last_as if unit == 0 else last_bs)[...] = acc.astype(bf16)
        if unit == 0:
            go_remote(last_as, last_ar, end_s.at[0], end_r.at[0], me.chip_peer)
        else:
            go_remote(last_bs, last_br, end_s.at[1], end_r.at[1], me.chip_peer)

    for t in range(more + 1):
        steps(0, t)
        if t == 0:
            small_spread()
        if t == more:
            finish(0)
        steps(1, t - 1)
    finish(1)
    arrived(last_ar, end_s.at[0], end_r.at[0])
    both = last_as[...].astype(f32) + last_ar[...].astype(f32)
    oq[:, cols(c, half_q)] = both[:, 0:half_q]
    oo[:, cols(c, half_o)] = both[:, half_q:wide]
    for k, ref, width in ((2, oq, half_q), (3, oo, half_o)):
        place = ref.at[:, cols(c, width)]
        go_remote(place, place, end_s.at[k], end_r.at[k], me.core_peer)
    acc = last_bs[...].astype(f32)
    oi[:, cols(c * 2 + x, quarter)] = acc[:, 0:quarter]
    ob[c * 2 + x] = acc[:, quarter : 2 * quarter]
    small_n[me.s] = small_x[me.s]
    for j in range(1, n):
        arrived(small_n.at[(me.s + n - j) % n], small_s.at[1 + j], small_r.at[1 + j])
    acc = small_n[0]
    for j in range(1, n):
        acc = acc + small_n[j]
    osm[...] = acc
    arrived(last_br, end_s.at[1], end_r.at[1])
    acc = last_br[...].astype(f32)
    oi[:, cols(c * 2 + 1 - x, quarter)] = acc[:, 0:quarter]
    ob[c * 2 + 1 - x] = acc[:, quarter : 2 * quarter]
    place = oi.at[:, cols(c, 2 * quarter)]
    go_remote(place, place, end_s.at[4], end_r.at[4], me.core_peer)
    place = ob.at[pl.ds(c * 2, 2)]
    go_remote(place, place, end_s.at[5], end_r.at[5], me.core_peer)
    for k, ref, width in ((2, oq, half_q), (3, oo, half_o), (4, oi, 2 * quarter)):
        arrived(ref.at[:, cols(1 - c, width)], end_s.at[k], end_r.at[k])
    arrived(ob.at[pl.ds((1 - c) * 2, 2)], end_s.at[5], end_r.at[5])
    for copy in pending:
        copy.wait_send()


def reduce_gradients(n, pairs, small):
    f32, bf16 = jnp.float32, jnp.bfloat16
    tokens = pairs[0][0].shape[0]
    turned = [left.T for left, _ in pairs]
    rows = turned[0].shape[0] // n
    turned = [a.reshape(n, rows, tokens) for a in turned[:3]] + [
        turned[3].reshape(n, 4, rows, tokens)
    ]
    grads = [right for _, right in pairs]
    operands = (*turned, *grads, small)
    quarter = grads[2].shape[1] // 4
    wide = (grads[0].shape[1] + grads[1].shape[1]) // 2
    shapes = [(rows, g.shape[1]) for g in grads[:3]] + [(4, rows, grads[3].shape[1]), small.shape[1:]]
    most = n // 2
    dma = pltpu.SemaphoreType.DMA
    vmem = pltpu.VMEM
    block = (rows, wide)
    outs = pl.pallas_call(
        functools.partial(reduce_kernel, n),
        out_shape=[jax.ShapeDtypeStruct(shape, f32) for shape in shapes],
        in_specs=[pl.BlockSpec(memory_space=pltpu.VMEM)] * 9,
        out_specs=[pl.BlockSpec(memory_space=pltpu.VMEM)] * 5,
        scratch_shapes=[
            vmem((n,) + block, bf16),
            vmem((n, 2, rows, 2 * quarter), bf16),
            vmem((n,) + block, bf16),
            vmem((n, 2, rows, 2 * quarter), bf16),
            vmem((n, rows, 2 * quarter), bf16),
            vmem((n, rows, 2 * quarter), bf16),
            vmem((2, most) + block, bf16),
            vmem((2, most, rows, 2 * quarter), bf16),
            vmem(block, bf16),
            vmem(block, bf16),
            vmem((rows, 2 * quarter), bf16),
            vmem((rows, 2 * quarter), bf16),
            vmem(small.shape, f32),
            vmem(small.shape, f32),
            vmem(small.shape, f32),
            dma((2, n)),
            dma((2, n)),
            dma((n,)),
            dma((n,)),
            dma((2, 2, most)),
            dma((2, 2, most)),
            dma((6,)),
            dma((6,)),
            dma((n + 1,)),
            dma((n + 1,)),
        ],
        compiler_params=pltpu.CompilerParams(
            collective_id=1, has_side_effects=True, vmem_limit_bytes=50 * 2**20
        ),
        name="reduce_gradients",
    )(*operands)
    outs = list(outs)
    outs[3] = outs[3].reshape(4 * rows, -1)
    return outs


def pack_small(parts, n):
    joined = jnp.concatenate([v.reshape(n, -1) for v in parts], 1)
    width = joined.shape[1]
    padded = -(-width // 2048) * 2048
    joined = jnp.pad(joined, ((0, 0), (0, padded - width)))
    return joined.reshape(n, padded // 128, 128)


def unpack_small(packed, sizes):
    flat = packed.reshape(packed.shape[0], -1)
    result, start = [], 0
    for size in sizes:
        result.append(flat[:, start : start + size].reshape(-1))
        start += size
    return result


def normalize(summed, gain_row, shift_row):
    average = jnp.mean(summed, -1, keepdims=True)
    centred = summed - average
    inv_scale = lax.rsqrt(jnp.mean(centred * centred, -1, keepdims=True) + EPSILON)
    unit_rows = centred * inv_scale
    return (
        unit_rows * gain_row.astype(jnp.float32) + shift_row.astype(jnp.float32),
        unit_rows,
        inv_scale,
    )


def norm_back(grad_unit, unit_rows, inv_scale):
    centred_grad = grad_unit - jnp.mean(grad_unit, -1, keepdims=True)
    return inv_scale * (
        centred_grad - unit_rows * jnp.mean(grad_unit * unit_rows, -1, keepdims=True)
    )


def head_probs(q_ref, k_ref, same, head):
    scores = lax.dot_general(
        q_ref[:, head], k_ref[:, head], (((1,), (1,)), ((), ())), preferred_element_type=jnp.float32
    ) * (1.0 / math.sqrt(HEAD_DIM))
    scores = jnp.where(same, scores, -1000000000.0)
    exponent = jnp.exp(scores - jnp.max(scores, -1, keepdims=True))
    return exponent / jnp.sum(exponent, -1, keepdims=True)


def attend_kernel(q_ref, k_ref, v_ref, down_ref, across_ref, mixed_ref):
    same = down_ref[...] == across_ref[...]
    for h in range(HEADS):
        head = slice(h * HEAD_DIM, (h + 1) * HEAD_DIM)
        probs = head_probs(q_ref, k_ref, same, head).astype(jnp.bfloat16)
        mixed_ref[:, head] = jnp.dot(
            probs, v_ref[:, head], preferred_element_type=jnp.float32
        ).astype(jnp.bfloat16)


def attend_back_kernel(q_ref, k_ref, v_ref, g_ref, down_ref, across_ref, out_ref):
    same = down_ref[...] == across_ref[...]
    scale = 1.0 / math.sqrt(HEAD_DIM)
    f32, bf16 = jnp.float32, jnp.bfloat16
    width = q_ref.shape[1]
    columns = (((0,), (0,)), ((), ()))
    for h in range(HEADS):
        start = h * HEAD_DIM
        head = slice(start, start + HEAD_DIM)
        probs = head_probs(q_ref, k_ref, same, head)
        grad = lax.dot_general(
            g_ref[:, head], v_ref[:, head], (((1,), (1,)), ((), ())), preferred_element_type=f32
        )
        row_dot = jnp.sum(probs * grad, -1, keepdims=True)
        grad = (probs * (grad - row_dot)).astype(bf16)
        out_ref[:, head] = (
            jnp.dot(grad, k_ref[:, head], preferred_element_type=f32) * scale
        ).astype(bf16)
        out_ref[:, width + start : width + start + HEAD_DIM] = (
            lax.dot_general(grad, q_ref[:, head], columns, preferred_element_type=f32) * scale
        ).astype(bf16)
        out_ref[:, 2 * width + start : 2 * width + start + HEAD_DIM] = lax.dot_general(
            probs.astype(bf16), g_ref[:, head], columns, preferred_element_type=f32
        ).astype(bf16)


def on_chip(kernel, shape, *operands):
    return pl.pallas_call(
        kernel,
        out_shape=jax.ShapeDtypeStruct(shape, jnp.bfloat16),
        in_specs=[pl.BlockSpec(memory_space=pltpu.VMEM)] * len(operands),
        out_specs=pl.BlockSpec(memory_space=pltpu.VMEM),
        compiler_params=pltpu.CompilerParams(vmem_limit_bytes=24 * 2**20),
    )(*operands)


def body(
    n_shard,
    n_rep,
    tokens,
    labels,
    w_qkv,
    bias_qv,
    w_out,
    bias_out,
    w_in,
    bias_in,
    w_back,
    bias_back,
    gain_one,
    shift_one,
    gain_two,
    shift_two,
    cotangent,
):
    vectors = (
        bias_qv,
        bias_out,
        bias_in,
        bias_back,
        gain_one,
        shift_one,
        gain_two,
        shift_two,
    )
    sizes = [v.shape[0] for v in vectors]
    full_qkv, full_out, full_in, full_back, packed = gather_weights(
        n_shard, w_qkv, w_out, w_in, w_back, pack_small(vectors, 1)[0]
    )
    (
        full_bias_qv,
        full_bias_out,
        full_bias_in,
        full_bias_back,
        full_gain_one,
        full_shift_one,
        full_gain_two,
        full_shift_two,
    ) = unpack_small(packed, sizes)
    model_width = full_out.shape[0]
    row_count = tokens.shape[0]
    qkv = jnp.dot(tokens, full_qkv, preferred_element_type=jnp.float32)
    bias_float = full_bias_qv.astype(jnp.float32)
    query_rows = (qkv[:, :model_width] + bias_float[:model_width]).astype(jnp.bfloat16)
    key_rows = qkv[:, model_width : 2 * model_width].astype(jnp.bfloat16)
    value_rows = (qkv[:, 2 * model_width :] + bias_float[model_width:]).astype(jnp.bfloat16)
    down, across = labels[:, None], labels[None, :]
    mixed_heads = on_chip(
        attend_kernel, query_rows.shape, query_rows, key_rows, value_rows, down, across
    )
    attn_out = jnp.dot(
        mixed_heads, full_out, preferred_element_type=jnp.float32
    ) + full_bias_out.astype(jnp.float32)
    first_out, unit_one, scale_one = normalize(
        tokens.astype(jnp.float32) + attn_out, full_gain_one, full_shift_one
    )
    first_low = first_out.astype(jnp.bfloat16)
    inner_sum = jnp.dot(
        first_low, full_in, preferred_element_type=jnp.float32
    ) + full_bias_in.astype(jnp.float32)
    share = 0.5 * (1.0 + lax.erf(inner_sum * math.sqrt(0.5)))
    slope = share + inner_sum * jnp.exp(-0.5 * inner_sum * inner_sum) / math.sqrt(2.0 * math.pi)
    activated, slope = lax.optimization_barrier(
        ((inner_sum * share).astype(jnp.bfloat16), slope)
    )
    branch = jnp.dot(
        activated, full_back, preferred_element_type=jnp.float32
    ) + full_bias_back.astype(jnp.float32)
    final_out, unit_two, scale_two = normalize(first_out + branch, full_gain_two, full_shift_two)
    live_rows = (labels > 0).astype(jnp.float32)[:, None]
    output = (final_out * live_rows).astype(jnp.bfloat16)
    grad_final = cotangent.astype(jnp.float32) * live_rows
    d_gain_two = jnp.sum(grad_final * unit_two, 0)
    d_shift_two = jnp.sum(grad_final, 0)
    grad_mid = norm_back(grad_final * full_gain_two.astype(jnp.float32), unit_two, scale_two)
    grad_branch = grad_mid.astype(jnp.bfloat16)
    d_bias_back = jnp.sum(grad_branch.astype(jnp.float32), 0)
    grad_act = jnp.einsum(
        "td,fd->tf", grad_branch, full_back, preferred_element_type=jnp.float32
    )
    grad_inner = (grad_act * slope).astype(jnp.bfloat16)
    d_bias_in = jnp.sum(grad_inner.astype(jnp.float32), 0)
    grad_first = (
        jnp.einsum("tf,df->td", grad_inner, full_in, preferred_element_type=jnp.float32) + grad_mid
    )
    d_gain_one = jnp.sum(grad_first * unit_one, 0)
    d_shift_one = jnp.sum(grad_first, 0)
    grad_res = norm_back(grad_first * full_gain_one.astype(jnp.float32), unit_one, scale_one)
    grad_attn = grad_res.astype(jnp.bfloat16)
    d_bias_out = jnp.sum(grad_attn.astype(jnp.float32), 0)
    grad_mixed = jnp.einsum(
        "te,de->td", grad_attn, full_out, preferred_element_type=jnp.float32
    ).astype(jnp.bfloat16)
    grad_qkv = on_chip(
        attend_back_kernel,
        (row_count, 3 * model_width),
        query_rows,
        key_rows,
        value_rows,
        grad_mixed,
        down,
        across,
    )
    grad_query = grad_qkv[:, :model_width]
    grad_values = grad_qkv[:, 2 * model_width :]
    d_bias_qv = jnp.concatenate(
        [jnp.sum(grad_query.astype(jnp.float32), 0), jnp.sum(grad_values.astype(jnp.float32), 0)], 0
    )
    grad_tokens = (
        jnp.einsum("te,de->td", grad_qkv, full_qkv, preferred_element_type=jnp.float32) + grad_res
    )
    pairs = (
        (tokens, grad_qkv),
        (mixed_heads, grad_attn),
        (first_low, grad_inner),
        (activated, grad_branch),
    )
    small_grads = pack_small(
        (
            d_bias_qv,
            d_bias_out,
            d_bias_in,
            d_bias_back,
            d_gain_one,
            d_shift_one,
            d_gain_two,
            d_shift_two,
        ),
        n_shard,
    )
    summed = reduce_gradients(n_shard, pairs, small_grads)
    if n_rep > QUAD:
        summed = [lax.psum(g, "rep") * (1.0 / QUAD) for g in summed]
    d_qkv, d_out, d_in, d_back, packed = summed
    vector = unpack_small(packed[None], sizes)
    return (
        output,
        grad_tokens,
        d_qkv,
        vector[0],
        d_out,
        vector[1],
        d_in,
        vector[2],
        d_back,
        vector[3],
        vector[4],
        vector[5],
        vector[6],
        vector[7],
    )


def solution(mesh):
    placed = (
        P(("shard", "rep"), None),
        P(("shard", "rep")),
        P("shard", None),
        P("shard"),
        P("shard", None),
        P("shard"),
        P("shard", None),
        P("shard"),
        P("shard", None),
        P("shard"),
        P("shard"),
        P("shard"),
        P("shard"),
        P("shard"),
        P(("shard", "rep"), None),
    )
    return jax.shard_map(
        functools.partial(body, mesh.shape["shard"], mesh.shape["rep"]),
        mesh=mesh,
        in_specs=placed,
        out_specs=(
            P(("shard", "rep"), None),
            P(("shard", "rep"), None),
            P("shard", None),
            P("shard"),
            P("shard", None),
            P("shard"),
            P("shard", None),
            P("shard"),
            P("shard", None),
            P("shard"),
            P("shard"),
            P("shard"),
            P("shard"),
            P("shard"),
        ),
        check_vma=False,
    )
```
